512 devices in a mesh: dp: 32 (over x, z_hi, core), tensor: 16 (over z_lo, y).
Axes of the slice: x: 4, y: 4, z: 16 (z_hi: 4, z_lo: 4; z = z_hi * 4 + z_lo), core: 2. Of those that a mesh axis runs over, the one named last changes fastest.
Arguments:
- prefill_states: bfloat16 [256, 2, 64, 128, 128], P('dp', None, 'tensor'), may hold values from -6 to 6
- prompt_slot: int32 [256], replicated, may hold values from 0 to 255, as said below
- sample_prompt: int32 [4096], P('dp'), may hold values from 0 to 255, as said below
- queries: bfloat16 [4096, 2, 2, 8192], P('dp', None, None, 'tensor'), may hold values from -2 to 2
- keys: bfloat16 [4096, 2, 2, 8192], P('dp', None, None, 'tensor'), may hold values from -3 to 3
- values: bfloat16 [4096, 2, 2, 8192], P('dp', None, None, 'tensor'), may hold values from -6 to 6
- gates: bfloat16 [4096, 2, 2, 8192], P('dp', None, None, 'tensor'), may hold values from -6 to 6
- norm_gain: float32 [2, 8192], P(None, 'tensor'), may hold values from 0.25 to 1.75
- decay_rate: float32 [2, 64], P(None, 'tensor'), may hold values from 0.01 to 1
Outputs:
- attended: float32 [4096, 2, 2, 8192], P('dp', None, None, 'tensor')
The draws below stay inside these ranges and needn't reach their ends.
Inputs may be any that keep to these rules, and one draw needn't show every extreme that they name: `prompt_slot`: A permutation: each slot holds one prompt; slot s lies with dp group s // 8. `sample_prompt`: rows g * 128 to (g + 1) * 128 - 1 hold, for r = 0 to 3, exactly 4 rows of each prompt whose slot lies with group (g - r * 8) modulo 256 / 8, in any order.
All inputs are finite; a program needn't handle non-finite values.
Results may differ from the reference program's by a relative error of at most 0.0003.
Values may be sent and summed in bfloat16 or wider, within the bound.
A program may use at most 64 MiB of HBM per device.

```python
import math
import jax
import jax.numpy as jnp
from jax import lax

HEADS = 64
HEAD_DIM = 128
LAYERS = 2
STEPS = 2
READERS = 4
SAMPLES_PER = 16
PR_DEV = 8
PROMPTS = 256
SAMPLES = 4096
QUARTER = 8


def slot_order(key):
    return jax.random.permutation(jax.random.fold_in(key, 101), PROMPTS).astype(jnp.int32)


def draw_prompt_slot(key, part):
    return slot_order(key)


def draw_sample_prompt(key, part):
    order = slot_order(key)
    prompt_at = jnp.zeros((PROMPTS,), jnp.int32).at[order].set(jnp.arange(PROMPTS, dtype=jnp.int32))
    groups = PROMPTS // PR_DEV
    reach = jnp.arange(READERS, dtype=jnp.int32)
    within = jnp.arange(PR_DEV, dtype=jnp.int32)
    copies = SAMPLES_PER // READERS
    shuffle_key = jax.random.fold_in(key, 202)

    def one_group(group):
        source = (group - reach * QUARTER) % groups
        slots = (source[:, None] * PR_DEV + within[None, :]).reshape(-1)
        slots = jnp.repeat(slots, copies)
        shuffled = jax.random.permutation(jax.random.fold_in(shuffle_key, group), slots)
        return prompt_at[shuffled]
    return jax.vmap(one_group)(jnp.arange(groups, dtype=jnp.int32)).reshape(-1).astype(jnp.int32)


def draw_queries(key, part):
    columns = HEADS * HEAD_DIM
    head = jnp.arange(columns) // HEAD_DIM
    rise = 3.0 ** (0.5 * head.astype(jnp.float32) / max(HEADS - 1, 1))
    head_factor = jnp.exp(jax.random.uniform(jax.random.fold_in(key, 7), (HEADS,), minval=0.0, maxval=math.log(3.2)))[head]
    shape = (SAMPLES, STEPS, LAYERS, columns)
    row_factor = jnp.exp(jax.random.uniform(jax.random.fold_in(key, 8), (SAMPLES, 1, 1, 1), minval=0.0, maxval=math.log(3.2)))
    base = jax.random.normal(jax.random.fold_in(key, 9), shape)
    drawn = base * HEAD_DIM ** (-0.5) * rise * head_factor * row_factor
    return jnp.clip(drawn, -2.0, 2.0).astype(jnp.bfloat16)


def steps_of(rng, dims, split, low, high):
    factor_of, own = 1.0, jax.random.fold_in(rng, 6)
    for axis_at, shards_of in split:
        heights = jnp.exp(jax.random.uniform(jax.random.fold_in(own, axis_at), (shards_of,), jnp.float32, low / len(split), high / len(split)))
        factor_of = factor_of * jnp.repeat(heights, dims[axis_at] // shards_of).reshape([-1 if axis == axis_at else 1 for axis in range(len(dims))])
    return factor_of


def bell_draw(key, extent, spread, bound, cuts=(), kind=jnp.bfloat16):
    values = spread * jax.random.normal(key, extent, jnp.float32)
    if cuts:
        values = values * steps_of(key, extent, cuts, -0.22, 0.18)
    return jnp.clip(values, -bound, bound).astype(kind)


def setup_inputs(seed: int = 0) -> dict:
    seeds = jax.random.split(jax.random.key(seed), 10)
    prefill_states = bell_draw(seeds[0], (PROMPTS, LAYERS, HEADS, HEAD_DIM, HEAD_DIM), 1.0, 6.0, ((0, 32), (2, 16)))
    prompt_slot = draw_prompt_slot(jax.random.fold_in(seeds[9], 71), 0)
    sample_prompt = draw_sample_prompt(jax.random.fold_in(seeds[9], 71), 0)
    queries = draw_queries(jax.random.fold_in(seeds[9], 71), 0)
    keys = bell_draw(seeds[4], (SAMPLES, STEPS, LAYERS, HEADS * HEAD_DIM), 0.5, 3.0, ((0, 32), (3, 16)))
    values = bell_draw(seeds[5], (SAMPLES, STEPS, LAYERS, HEADS * HEAD_DIM), 1.0, 6.0, ((0, 32), (3, 16)))
    gates = bell_draw(seeds[6], (SAMPLES, STEPS, LAYERS, HEADS * HEAD_DIM), 1.0, 6.0, ((0, 32), (3, 16)))
    norm_gain = jnp.clip(1.0 + 0.15 * jax.random.normal(seeds[7], (LAYERS, HEADS * HEAD_DIM), jnp.float32), 0.25, 1.75)
    decay_rate = jnp.clip(jnp.exp(math.log(1.0) - 4.6051702 * jax.random.uniform(seeds[8], (LAYERS, HEADS), jnp.float32) ** steps_of(seeds[8], (LAYERS, HEADS), ((1, 16),), -0.2, 0.2)), 0.01, 1.0)
    return dict(prefill_states=prefill_states, prompt_slot=prompt_slot, sample_prompt=sample_prompt, queries=queries, keys=keys, values=values, gates=gates, norm_gain=norm_gain, decay_rate=decay_rate)


def reference(prefill_states, prompt_slot, sample_prompt, queries, keys, values, gates, norm_gain, decay_rate):
    retain = jnp.exp(-decay_rate)[None, :, :, None]
    shape = (SAMPLES, STEPS, LAYERS, HEADS, HEAD_DIM)
    query_all = queries.astype(jnp.float32).reshape(shape)
    key_all = keys.astype(jnp.float32).reshape(shape)
    value_all = values.astype(jnp.float32).reshape(shape)
    slots = prompt_slot[sample_prompt].astype(jnp.int32)

    def one_row(pair):
        slot, query_row = pair
        state = prefill_states[slot].astype(jnp.float32)
        return jnp.einsum('jlhd,lhde->jlhe', query_row, state, precision=lax.Precision.HIGHEST)
    reach = lax.map(one_row, (slots, query_all))
    first_first = lax.optimization_barrier(jnp.sum(query_all[:, 0] * key_all[:, 0], axis=-1))[..., None]
    second_first = lax.optimization_barrier(jnp.sum(query_all[:, 1] * key_all[:, 0], axis=-1))[..., None]
    second_second = lax.optimization_barrier(jnp.sum(query_all[:, 1] * key_all[:, 1], axis=-1))[..., None]
    out_one = retain * reach[:, 0] + first_first * value_all[:, 0]
    out_two = retain * retain * reach[:, 1] + retain * second_first * value_all[:, 0] + second_second * value_all[:, 1]
    mixed = jnp.stack([out_one, out_two], axis=1).reshape(SAMPLES, STEPS, LAYERS, HEADS * HEAD_DIM)
    total = lax.optimization_barrier(jnp.sum(mixed * mixed, axis=-1))
    scale = lax.rsqrt(total / (HEADS * HEAD_DIM) + 1e-05)
    return mixed * scale[..., None] * norm_gain[None, None] * jax.nn.sigmoid(gates.astype(jnp.float32))
```

```python
import functools

import jax
import jax.numpy as jnp
from jax import lax
from jax.experimental import pallas as pl
from jax.experimental.pallas import tpu as pltpu
from jax.sharding import PartitionSpec as P

STEPS = 2
LAYERS = 2
READERS = 4
CHUNKS = 2
LANES = 128
TOP = 32767.0
FINE = 256.0
MESH = pl.DeviceIdType.MESH
F32, BF16, I32, I16 = jnp.float32, jnp.bfloat16, jnp.int32, jnp.int16


def iota(shape, axis):
    return lax.broadcasted_iota(I32, shape, axis)


def places(group, groups, owned, copies, sample_prompt, prompt_slot):
    prompts, rows = prompt_slot.shape[1], sample_prompt.shape[1]
    match = (iota((prompts, rows), 0) == sample_prompt).astype(F32).astype(BF16)
    slot_row = jnp.broadcast_to(prompt_slot.astype(F32), (8, prompts)).astype(BF16)
    slots = jnp.dot(slot_row, match, preferred_element_type=F32).astype(I32)[0:1]
    owner, within = slots // owned, slots % owned
    reach = ((group - owner + groups) % groups) // (groups // READERS)
    candidate = reach * owned + within
    count = READERS * owned
    mine = iota((count, rows), 0) == candidate
    earlier = (iota((rows, rows), 0) < iota((rows, rows), 1)).astype(F32).astype(BF16)
    before = jnp.dot(mine.astype(F32).astype(BF16), earlier, preferred_element_type=F32)
    rank = jnp.sum(jnp.where(mine, before, 0.0), axis=0, keepdims=True).astype(I32)
    place = jnp.clip(candidate * copies + rank, 0, rows - 1)
    at = (iota((rows, rows), 0) == place).astype(F32).astype(BF16)
    number = iota((8, rows), 1).astype(F32).astype(BF16)
    order = lax.dot_general(number, at, (((1,), (1,)), ((), ())), preferred_element_type=F32)
    order = jnp.clip(order.astype(I32), 0, rows - 1)
    return jnp.where(iota((8, rows), 0) == 0, order, jnp.broadcast_to(place, (8, rows)))


def kernel(
    groups,
    shards,
    states_hbm,
    slot_hbm,
    prompt_hbm,
    queries_hbm,
    keys_hbm,
    values_hbm,
    gates_hbm,
    gain_hbm,
    decay_ref,
    out_ref,
    states,
    slot_row,
    prompt_row,
    queries,
    rest,
    gain,
    index_vmem,
    index,
    sorted_q,
    arrived_q,
    spread_q,
    products,
    codes_out,
    codes_in,
    local_part,
    gated,
    mixed,
    squares,
    small_sem,
    big_sem,
    query_send,
    query_recv,
    code_send,
    code_recv,
    square_send,
    square_recv,
):
    group, shard = lax.axis_index("dp"), lax.axis_index("tensor")
    quarter = groups // READERS
    owned, layers, heads = states.shape[:3]
    rows, tile = queries.shape[:2]
    pairs = heads * layers
    block = rows // READERS
    part = block // CHUNKS
    copies = block // owned
    part_prompts = owned // CHUNKS

    def reader(r):
        return (lax.rem(group + quarter * r, groups), shard)

    others = [(group, lax.rem(shard + k, shards)) for k in range(1, shards)]

    first = [
        pltpu.make_async_copy(prompt_hbm, prompt_row, small_sem.at[0]),
        pltpu.make_async_copy(slot_hbm, slot_row, small_sem.at[1]),
    ]
    take_q = pltpu.make_async_copy(queries_hbm, queries, big_sem.at[0])
    take_states = pltpu.make_async_copy(states_hbm, states, big_sem.at[1])
    later = [
        pltpu.make_async_copy(ref, rest.at[n], big_sem.at[2 + n])
        for n, ref in enumerate((keys_hbm, values_hbm, gates_hbm))
    ]
    take_gain = pltpu.make_async_copy(gain_hbm, gain, small_sem.at[2])
    for copy in (*first, take_q, take_states, *later, take_gain):
        copy.start()

    barrier = pltpu.get_barrier_semaphore()
    met = [reader(r) for r in range(1, READERS)] + others
    for device in met:
        pl.semaphore_signal(barrier, inc=1, device_id=device, device_id_type=MESH)

    for copy in first:
        copy.wait()
    index_vmem[...] = places(group, groups, owned, copies, prompt_row[...], slot_row[...])
    take_index = pltpu.make_async_copy(index_vmem, index, small_sem.at[0])
    take_index.start()
    take_index.wait()
    take_q.wait()

    def at_index(which, n):
        return jnp.clip(index[which, n], 0, rows - 1)

    def gather(start, count):
        def step(n, carry):
            sorted_q[start + n] = queries[at_index(0, start + n)]
            return carry

        lax.fori_loop(0, count, step, 0, unroll=8)

    def query_copy(r, c):
        return pltpu.make_async_remote_copy(
            src_ref=sorted_q.at[pl.ds(r * block + c * part, part)],
            dst_ref=arrived_q.at[r - 1, pl.ds(c * part, part)],
            send_sem=query_send,
            recv_sem=query_recv.at[r - 1, c],
            device_id=reader(READERS - r),
            device_id_type=MESH,
        )

    def code_copy(r, c):
        return pltpu.make_async_remote_copy(
            src_ref=codes_out.at[r - 1, c],
            dst_ref=codes_in.at[r - 1, c],
            send_sem=code_send,
            recv_sem=code_recv.at[r - 1, c],
            device_id=reader(r),
            device_id_type=MESH,
        )

    hops = (1, 3, 2)
    met_all = False
    for c in range(CHUNKS):
        for r in hops:
            gather(r * block + c * part, part)
            if not met_all:
                pl.semaphore_wait(barrier, len(met))
                met_all = True
            query_copy(r, c).start()
    gather(0, block)

    def multiply(blocks, c):
        size = copies * tile
        for n, ref in enumerate(blocks):
            wide = ref[...].astype(F32).reshape(part * tile, LANES)
            spread_q[n, pl.ds(0, part * tile)] = wide

        def step(p, carry):
            for pair in range(pairs):
                left = [
                    spread_q[n, pl.ds(p * size + pair, copies * STEPS, stride=pairs), :]
                    for n in range(len(blocks))
                ]
                left = jnp.concatenate(left, axis=0) if len(left) > 1 else left[0]
                state = states[c * part_prompts + p, pair % layers, pair // layers]
                answer = jnp.dot(left.astype(BF16), state, preferred_element_type=F32)
                for n in range(len(blocks)):
                    products[n, pl.ds(p * size + pair, copies * STEPS, stride=pairs), :] = answer[
                        n * copies * STEPS : (n + 1) * copies * STEPS
                    ]
            return carry

        lax.fori_loop(0, part_prompts, step, 0)

    lane = iota((tile, LANES), 1)

    def encode(n, r, c):
        def step(j, scales):
            here = products[n, pl.ds(pl.multiple_of(j * tile, tile), tile), :]
            most = jnp.maximum(jnp.max(jnp.abs(here), axis=1, keepdims=True), 1e-30)
            scale = jnp.ceil(jnp.log2(most) * FINE + 0.25)
            code = jnp.round(here * (jnp.exp2(scale * (-1.0 / FINE)) * TOP))
            codes_out[r - 1, c, j] = code.astype(I32).astype(I16)
            return jnp.where(lane == j, scale, scales)

        scales = lax.fori_loop(0, part, step, jnp.zeros((tile, LANES), F32), unroll=4)
        codes_out[r - 1, c, part] = scales.astype(I32).astype(I16)

    row = iota((pairs, LANES), 0)
    decay = jnp.zeros((pairs, LANES), F32)
    for pair in range(pairs):
        decay = jnp.where(row == pair, decay_ref[pair % layers, pair // layers], decay)
    retain = jnp.exp(-decay)
    kept = jnp.concatenate([retain, retain * retain], axis=0)

    def add_up(j, total, sums):
        mixed[j] = total
        square = jnp.sum(total * total, axis=1, keepdims=True)
        return jnp.where(lane == j, square, sums)

    for copy in later:
        copy.wait()
    take_gain.wait()

    def terms(j, carry):
        at = at_index(0, j)
        query = sorted_q[j].astype(F32)
        key, value, gate = (rest[n, at].astype(F32) for n in range(3))
        one, two = slice(0, pairs), slice(pairs, tile)
        first_first = jnp.sum(query[one] * key[one], axis=1, keepdims=True)
        second_first = jnp.sum(query[two] * key[one], axis=1, keepdims=True)
        second_second = jnp.sum(query[two] * key[two], axis=1, keepdims=True)
        local_part[j, one] = first_first * value[one]
        local_part[j, two] = (second_first * retain) * value[one] + second_second * value[two]
        gains = jnp.concatenate([gain[...], gain[...]], axis=0)
        gated[j] = gains * jax.nn.sigmoid(gate)
        return carry

    lax.fori_loop(0, rows, terms, 0, unroll=4)

    take_states.wait()
    sums = jnp.zeros((tile, LANES), F32)
    for c in range(CHUNKS):
        multiply([sorted_q.at[pl.ds(c * part, part)]], c)

        def own(j, sums):
            reach = products[0, pl.ds(pl.multiple_of(j * tile, tile), tile), :]
            at = c * part + j
            return add_up(at, kept * reach + local_part[at], sums)

        sums = lax.fori_loop(0, part, own, sums, unroll=4)

    for c in range(CHUNKS):
        for some in ((1, 3), (2,)):
            for r in some:
                query_copy(r, c).wait_recv()
            multiply([arrived_q.at[r - 1, pl.ds(c * part, part)] for r in some], c)
            for n, r in enumerate(some):
                encode(n, r, c)
                code_copy(r, c).start()

    for c in range(CHUNKS):
        for r in hops:
            code_copy(r, c).wait_recv()
            scales = jnp.exp2(codes_in[r - 1, c, part].astype(I32).astype(F32) * (1.0 / FINE))
            scales = scales * (1.0 / TOP) * kept

            def decode(j, sums):
                at = r * block + c * part + j
                scale = jnp.sum(jnp.where(lane == j, scales, 0.0), axis=1, keepdims=True)
                reach = codes_in[r - 1, c, j].astype(I32).astype(F32) * scale
                return add_up(at, reach + local_part[at], sums)

            sums = lax.fori_loop(0, part, decode, sums, unroll=4)

    total = []
    for t in range(STEPS):
        here = sums[t * pairs : (t + 1) * pairs]
        for n in (pairs // 2, pairs // 4):
            here = here + pltpu.roll(here, n, 0)
        total.append(here)
    late = (row // layers) % STEPS == 1
    squares[0] = jnp.where(late, total[1], total[0])
    sends = []
    for k, device in enumerate(others):
        copy = pltpu.make_async_remote_copy(
            src_ref=squares.at[0],
            dst_ref=squares.at[k + 1],
            send_sem=square_send,
            recv_sem=square_recv,
            device_id=device,
            device_id_type=MESH,
        )
        copy.start()
    all_but_one = squares.at[pl.ds(1, shards - 1)]
    pltpu.make_async_copy(all_but_one, all_but_one, square_recv).wait()
    whole = squares[0]
    for k in range(1, shards):
        whole = whole + squares[k]
    scale = lax.rsqrt(whole / (shards * heads * LANES) + 1e-05)
    other = pltpu.roll(scale, layers, 0)
    scale = jnp.concatenate([jnp.where(late, other, scale), jnp.where(late, scale, other)], axis=0)

    def finish(j, carry):
        norm = jnp.sum(jnp.where(lane == j, scale, 0.0), axis=1, keepdims=True)
        mixed[j] = mixed[j] * norm * gated[j]
        return carry

    lax.fori_loop(0, rows, finish, 0, unroll=4)

    def place_back(n, carry):
        out_ref[n] = mixed[at_index(1, n)]
        return carry

    lax.fori_loop(0, rows, place_back, 0, unroll=8)

    pltpu.make_async_copy(all_but_one, all_but_one, square_send).wait()
    pltpu.make_async_copy(arrived_q, arrived_q, query_send).wait()
    pltpu.make_async_copy(codes_in, codes_in, code_send).wait()


def tiles(array, rows, heads):
    array = array.reshape(rows, STEPS, LAYERS, heads, LANES).transpose(0, 1, 3, 2, 4)
    return array.reshape(rows, STEPS * heads * LAYERS, LANES)


def local(
    prefill_states, prompt_slot, sample_prompt, queries, keys, values, gates, norm_gain, decay_rate
):
    groups, shards = lax.axis_size("dp"), lax.axis_size("tensor")
    owned, layers, heads = prefill_states.shape[:3]
    rows = sample_prompt.shape[0]
    tile = STEPS * heads * layers
    block = rows // READERS
    part = block // CHUNKS
    prompts = prompt_slot.shape[0]
    gain = norm_gain.reshape(layers, heads, LANES).transpose(1, 0, 2).reshape(heads * layers, LANES)
    hbm = pl.BlockSpec(memory_space=pltpu.HBM)
    vmem = pltpu.VMEM
    dma = pltpu.SemaphoreType.DMA
    out = pl.pallas_call(
        functools.partial(kernel, groups, shards),
        out_shape=jax.ShapeDtypeStruct((rows, tile, LANES), F32),
        in_specs=[hbm] * 8 + [pl.BlockSpec(memory_space=pltpu.SMEM)],
        out_specs=pl.BlockSpec(memory_space=pltpu.VMEM),
        scratch_shapes=[
            vmem(prefill_states.shape, BF16),
            vmem((1, prompts), I32),
            vmem((1, rows), I32),
            vmem((rows, tile, LANES), BF16),
            vmem((3, rows, tile, LANES), BF16),
            vmem((heads * layers, LANES), F32),
            vmem((8, rows), I32),
            pltpu.SMEM((8, rows), I32),
            vmem((rows, tile, LANES), BF16),
            vmem((READERS - 1, block, tile, LANES), BF16),
            vmem((2, part * tile + heads * layers * LAYERS * STEPS * 2, LANES), F32),
            vmem((2, part * tile + heads * layers * LAYERS * STEPS * 2, LANES), F32),
            vmem((READERS - 1, CHUNKS, part + 1, tile, LANES), I16),
            vmem((READERS - 1, CHUNKS, part + 1, tile, LANES), I16),
            vmem((rows, tile, LANES), F32),
            vmem((rows, tile, LANES), F32),
            vmem((rows, tile, LANES), F32),
            vmem((shards, heads * layers, LANES), F32),
            dma((3,)),
            dma((5,)),
            dma,
            dma((READERS - 1, CHUNKS)),
            dma,
            dma((READERS - 1, CHUNKS)),
            dma,
            dma,
        ],
        compiler_params=pltpu.CompilerParams(
            collective_id=0, has_side_effects=True, vmem_limit_bytes=56 * 2**20
        ),
        cost_estimate=pl.CostEstimate(flops=2**26, bytes_accessed=5 * 2**20, transcendentals=2**19),
    )(
        prefill_states,
        prompt_slot.reshape(1, prompts),
        sample_prompt.reshape(1, rows),
        tiles(queries, rows, heads),
        tiles(keys, rows, heads),
        tiles(values, rows, heads),
        tiles(gates, rows, heads),
        gain,
        decay_rate,
    )
    out = out.reshape(rows, STEPS, heads, LAYERS, LANES).transpose(0, 1, 3, 2, 4)
    return out.reshape(rows, STEPS, LAYERS, heads * LANES)


def solution(mesh):
    return jax.shard_map(
        local,
        mesh=mesh,
        in_specs=(
            P("dp", None, "tensor", None, None),
            P(),
            P("dp"),
            P("dp", None, None, "tensor"),
            P("dp", None, None, "tensor"),
            P("dp", None, None, "tensor"),
            P("dp", None, None, "tensor"),
            P(None, "tensor"),
            P(None, "tensor"),
        ),
        out_specs=P("dp", None, None, "tensor"),
        check_vma=False,
    )
```

```python
import functools

import jax
import jax.numpy as jnp
from jax import lax
from jax.experimental import pallas as pl
from jax.experimental.pallas import tpu as pltpu
from jax.sharding import PartitionSpec as P

STEPS = 2
LAYERS = 2
READERS = 4
CHUNKS = 2
LANES = 128
TOP = 32767.0
FINE = 256.0
BATCH = 4
MESH = pl.DeviceIdType.MESH
F32, BF16, I32, I16 = jnp.float32, jnp.bfloat16, jnp.int32, jnp.int16


def iota(shape, axis):
    return lax.broadcasted_iota(I32, shape, axis)


def places(group, groups, owned, copies, sample_prompt, prompt_slot):
    prompts, rows = prompt_slot.shape[1], sample_prompt.shape[1]
    match = (iota((prompts, rows), 0) == sample_prompt).astype(F32).astype(BF16)
    slot_row = jnp.broadcast_to(prompt_slot.astype(F32), (8, prompts)).astype(BF16)
    slots = jnp.dot(slot_row, match, preferred_element_type=F32).astype(I32)[0:1]
    owner, within = slots // owned, slots % owned
    reach = ((group - owner + groups) % groups) // (groups // READERS)
    candidate = reach * owned + within
    count = READERS * owned
    mine = iota((count, rows), 0) == candidate
    earlier = (iota((rows, rows), 0) < iota((rows, rows), 1)).astype(F32).astype(BF16)
    before = jnp.dot(mine.astype(F32).astype(BF16), earlier, preferred_element_type=F32)
    rank = jnp.sum(jnp.where(mine, before, 0.0), axis=0, keepdims=True).astype(I32)
    place = jnp.clip(candidate * copies + rank, 0, rows - 1)
    at = (iota((rows, rows), 0) == place).astype(F32).astype(BF16)
    number = iota((8, rows), 1).astype(F32).astype(BF16)
    order = lax.dot_general(number, at, (((1,), (1,)), ((), ())), preferred_element_type=F32)
    order = jnp.clip(order.astype(I32), 0, rows - 1)
    return jnp.where(iota((8, rows), 0) == 0, order, jnp.broadcast_to(place, (8, rows)))


def kernel(
    groups,
    shards,
    states_hbm,
    slot_hbm,
    prompt_hbm,
    queries_hbm,
    keys_hbm,
    values_hbm,
    gates_hbm,
    gain_hbm,
    decay_hbm,
    out_ref,
    states,
    slot_row,
    prompt_row,
    queries,
    rest,
    gain,
    index_vmem,
    index,
    decay_ref,
    sorted_q,
    arrived_q,
    spread_q,
    products,
    codes_out,
    codes_in,
    local_part,
    gated,
    mixed,
    squares,
    small_sem,
    big_sem,
    query_send,
    query_recv,
    code_send,
    code_recv,
    square_send,
    square_recv,
):
    group, shard = lax.axis_index("dp"), lax.axis_index("tensor")
    quarter = groups // READERS
    owned, layers, heads = states.shape[:3]
    rows, tile = queries.shape[:2]
    pairs = heads * layers
    block = rows // READERS
    part = block // CHUNKS
    copies = block // owned
    part_prompts = owned // CHUNKS

    def reader(r):
        return (lax.rem(group + quarter * r, groups), shard)

    others = [(group, lax.rem(shard + k, shards)) for k in range(1, shards)]

    first = [
        pltpu.make_async_copy(prompt_hbm, prompt_row, small_sem.at[0]),
        pltpu.make_async_copy(slot_hbm, slot_row, small_sem.at[1]),
    ]
    take_q = pltpu.make_async_copy(queries_hbm, queries, big_sem.at[0])
    take_states = pltpu.make_async_copy(states_hbm, states, big_sem.at[1])
    later = [
        pltpu.make_async_copy(ref, rest.at[n], big_sem.at[2 + n])
        for n, ref in enumerate((keys_hbm, values_hbm, gates_hbm))
    ]
    take_gain = pltpu.make_async_copy(gain_hbm, gain, small_sem.at[2])
    take_decay = pltpu.make_async_copy(decay_hbm, decay_ref, small_sem.at[3])
    for copy in (*first, take_q, take_states, *later, take_gain, take_decay):
        copy.start()

    barrier = pltpu.get_barrier_semaphore()
    met = [reader(r) for r in range(1, READERS)] + others
    for device in met:
        pl.semaphore_signal(barrier, inc=1, device_id=device, device_id_type=MESH)

    for copy in first:
        copy.wait()
    index_vmem[...] = places(group, groups, owned, copies, prompt_row[...], slot_row[...])
    take_index = pltpu.make_async_copy(index_vmem, index, small_sem.at[0])
    take_index.start()
    take_index.wait()
    take_q.wait()

    def at_index(which, n):
        return jnp.clip(index[which, n], 0, rows - 1)

    def gather(start, count):
        def step(n, carry):
            sorted_q[start + n] = queries[at_index(0, start + n)]
            return carry

        lax.fori_loop(0, count, step, 0, unroll=8)

    def query_copy(r, c):
        return pltpu.make_async_remote_copy(
            src_ref=sorted_q.at[pl.ds(r * block + c * part, part)],
            dst_ref=arrived_q.at[r - 1, pl.ds(c * part, part)],
            send_sem=query_send,
            recv_sem=query_recv.at[r - 1, c],
            device_id=reader(READERS - r),
            device_id_type=MESH,
        )

    def code_copy(r, c):
        return pltpu.make_async_remote_copy(
            src_ref=codes_out.at[r - 1, c],
            dst_ref=codes_in.at[r - 1, c],
            send_sem=code_send,
            recv_sem=code_recv.at[r - 1, c],
            device_id=reader(r),
            device_id_type=MESH,
        )

    hops = (1, 3, 2)
    met_all = False
    for c in range(CHUNKS):
        for r in hops:
            gather(r * block + c * part, part)
            if not met_all:
                pl.semaphore_wait(barrier, len(met))
                met_all = True
            query_copy(r, c).start()
    gather(0, block)

    def multiply(blocks, c):
        size = copies * tile
        for n, ref in enumerate(blocks):
            wide = ref[...].astype(F32).reshape(part * tile, LANES)
            spread_q[n, pl.ds(0, part * tile)] = wide

        for p in range(part_prompts):
            for pair in range(pairs):
                some = pl.ds(p * size + pair, copies * STEPS, stride=pairs)
                left = [spread_q[n, some, :] for n in range(len(blocks))]
                left = jnp.concatenate(left, axis=0) if len(left) > 1 else left[0]
                state = states[c * part_prompts + p, pair % layers, pair // layers]
                answer = jnp.dot(left.astype(BF16), state, preferred_element_type=F32)
                for n in range(len(blocks)):
                    products[n, some, :] = answer[n * copies * STEPS : (n + 1) * copies * STEPS]

    height = BATCH * tile
    lane = iota((tile, LANES), 1)
    skew = jnp.concatenate([lane - n for n in range(BATCH)], axis=0)
    ones = jnp.ones((2 * LANES, LANES), F32).astype(BF16)

    def row_sums(wide):
        high = wide.astype(BF16)
        low = (wide - high.astype(F32)).astype(BF16)
        return jnp.dot(jnp.concatenate([high, low], axis=1), ones, preferred_element_type=F32)

    def spread(columns, j):
        many = jnp.concatenate([columns] * BATCH, axis=0)
        return row_sums(jnp.where(skew == j, many, 0.0))

    def over_tiles(wide):
        return sum(wide[n * tile : (n + 1) * tile] for n in range(BATCH))

    def batches(count, step, carry):
        return lax.fori_loop(0, count // BATCH, lambda b, had: step(b * BATCH, had), carry, unroll=2)

    def some_products(n, j):
        return products[n, pl.ds(pl.multiple_of(j * tile, height), height), :]

    def encode(n, r, c):
        def step(j, scales):
            here = some_products(n, j)
            most = jnp.maximum(jnp.max(jnp.abs(here), axis=1, keepdims=True), 1e-30)
            scale = jnp.ceil(jnp.log2(most) * FINE + 0.25)
            code = jnp.round(here * (jnp.exp2(scale * (-1.0 / FINE)) * TOP))
            code = code.astype(I32).astype(I16)
            codes_out[r - 1, c, pl.ds(j, BATCH)] = code.reshape(BATCH, tile, LANES)
            return scales + over_tiles(jnp.where(skew == j, scale, 0.0))

        scales = batches(part, step, jnp.zeros((tile, LANES), F32))
        codes_out[r - 1, c, part] = scales.astype(I32).astype(I16)

    take_decay.wait()
    row = iota((pairs, LANES), 0)
    decay = jnp.zeros((pairs, LANES), F32)
    for pair in range(pairs):
        decay = jnp.where(row == pair, decay_ref[pair % layers, pair // layers], decay)
    retain = jnp.exp(-decay)
    kept = jnp.concatenate([retain, retain * retain], axis=0)
    retains = jnp.concatenate([retain] * BATCH, axis=0)
    kept_batch = jnp.concatenate([kept] * BATCH, axis=0)

    def add_up(j, reach, sums):
        total = reach + local_part[pl.ds(j, BATCH)].reshape(height, LANES)
        mixed[pl.ds(j, BATCH)] = total.reshape(BATCH, tile, LANES)
        square = row_sums(total * total)
        for n in range(BATCH):
            here = square[n * tile : (n + 1) * tile]
            sums = jnp.where(lane == at_index(0, j + n), here, sums)
        return sums

    for copy in later:
        copy.wait()
    take_gain.wait()

    def terms(j, carry):
        query = sorted_q[pl.ds(j, BATCH)].astype(F32)
        key, value = (
            jnp.stack([rest[m, at_index(0, j + n)] for n in range(BATCH)]).astype(F32)
            for m in range(2)
        )

        def of(wide, t):
            return wide[:, t * pairs : (t + 1) * pairs].reshape(BATCH * pairs, LANES)

        key_one, value_one = of(key, 0), of(value, 0)
        inner = jnp.concatenate(
            [of(query, 0) * key_one, of(query, 1) * key_one, of(query, 1) * of(key, 1)], axis=0
        )
        inner = row_sums(inner).reshape(3, BATCH * pairs, LANES)
        term_one = inner[0] * value_one
        term_two = inner[1] * retains * value_one + inner[2] * of(value, 1)
        shape = (BATCH, pairs, LANES)
        local_part[pl.ds(j, BATCH), 0:pairs] = term_one.reshape(shape)
        local_part[pl.ds(j, BATCH), pairs:tile] = term_two.reshape(shape)
        gate = rest[2, pl.ds(j, BATCH)].astype(F32)
        gated[pl.ds(j, BATCH)] = gains[None] * jax.nn.sigmoid(gate)
        return carry

    gains = jnp.concatenate([gain[...], gain[...]], axis=0)
    batches(rows, terms, 0)

    take_states.wait()
    sums = jnp.zeros((tile, LANES), F32)
    for c in range(CHUNKS):
        multiply([sorted_q.at[pl.ds(c * part, part)]], c)

        def own(j, sums):
            return add_up(c * part + j, kept_batch * some_products(0, j), sums)

        sums = batches(part, own, sums)

    for c in range(CHUNKS):
        for some in ((1, 3), (2,)):
            for r in some:
                query_copy(r, c).wait_recv()
            multiply([arrived_q.at[r - 1, pl.ds(c * part, part)] for r in some], c)
            for n, r in enumerate(some):
                encode(n, r, c)
                code_copy(r, c).start()

    for c in range(CHUNKS):
        for r in hops:
            code_copy(r, c).wait_recv()
            scales = jnp.exp2(codes_in[r - 1, c, part].astype(I32).astype(F32) * (1.0 / FINE))
            scales = scales * (1.0 / TOP) * kept

            def decode(j, sums):
                code = codes_in[r - 1, c, pl.ds(j, BATCH)].astype(I32).astype(F32)
                reach = code.reshape(height, LANES) * spread(scales, j)
                return add_up(r * block + c * part + j, reach, sums)

            sums = batches(part, decode, sums)

    total = []
    for t in range(STEPS):
        here = sums[t * pairs : (t + 1) * pairs]
        for n in (pairs // 2, pairs // 4):
            here = here + pltpu.roll(here, n, 0)
        total.append(here)
    late = (row // layers) % STEPS == 1
    squares[0] = jnp.where(late, total[1], total[0])
    sends = []
    for k, device in enumerate(others):
        copy = pltpu.make_async_remote_copy(
            src_ref=squares.at[0],
            dst_ref=squares.at[k + 1],
            send_sem=square_send,
            recv_sem=square_recv,
            device_id=device,
            device_id_type=MESH,
        )
        copy.start()
    all_but_one = squares.at[pl.ds(1, shards - 1)]
    pltpu.make_async_copy(all_but_one, all_but_one, square_recv).wait()
    whole = squares[0]
    for k in range(1, shards):
        whole = whole + squares[k]
    scale = lax.rsqrt(whole / (shards * heads * LANES) + 1e-05)
    other = pltpu.roll(scale, layers, 0)
    scale = jnp.concatenate([jnp.where(late, other, scale), jnp.where(late, scale, other)], axis=0)

    def finish(j, carry):
        here = jnp.stack([mixed[at_index(1, j + n)] for n in range(BATCH)])
        norm = spread(scale, j).reshape(BATCH, tile, LANES)
        out_ref[pl.ds(j, BATCH)] = here * norm * gated[pl.ds(j, BATCH)]
        return carry

    batches(rows, finish, 0)

    pltpu.make_async_copy(all_but_one, all_but_one, square_send).wait()
    pltpu.make_async_copy(arrived_q, arrived_q, query_send).wait()
    pltpu.make_async_copy(codes_in, codes_in, code_send).wait()


def tiles(array, rows, heads):
    array = array.reshape(rows, STEPS, LAYERS, heads, LANES).transpose(0, 1, 3, 2, 4)
    return array.reshape(rows, STEPS * heads * LAYERS, LANES)


def local(
    prefill_states, prompt_slot, sample_prompt, queries, keys, values, gates, norm_gain, decay_rate
):
    groups, shards = lax.axis_size("dp"), lax.axis_size("tensor")
    owned, layers, heads = prefill_states.shape[:3]
    rows = sample_prompt.shape[0]
    tile = STEPS * heads * layers
    block = rows // READERS
    part = block // CHUNKS
    prompts = prompt_slot.shape[0]
    gain = norm_gain.reshape(layers, heads, LANES).transpose(1, 0, 2).reshape(heads * layers, LANES)
    hbm = pl.BlockSpec(memory_space=pl.ANY)
    vmem = pltpu.VMEM
    dma = pltpu.SemaphoreType.DMA
    out = pl.pallas_call(
        functools.partial(kernel, groups, shards),
        out_shape=jax.ShapeDtypeStruct((rows, tile, LANES), F32),
        in_specs=[hbm] * 9,
        out_specs=pl.BlockSpec(memory_space=pltpu.VMEM),
        scratch_shapes=[
            vmem(prefill_states.shape, BF16),
            vmem((1, prompts), I32),
            vmem((1, rows), I32),
            vmem((rows, tile, LANES), BF16),
            vmem((3, rows, tile, LANES), BF16),
            vmem((heads * layers, LANES), F32),
            vmem((8, rows), I32),
            pltpu.SMEM((8, rows), I32),
            pltpu.SMEM(decay_rate.shape, F32),
            vmem((rows, tile, LANES), BF16),
            vmem((READERS - 1, block, tile, LANES), BF16),
            vmem((2, part * tile + heads * layers * LAYERS * STEPS * 2, LANES), F32),
            vmem((2, part * tile + heads * layers * LAYERS * STEPS * 2, LANES), F32),
            vmem((READERS - 1, CHUNKS, part + 1, tile, LANES), I16),
            vmem((READERS - 1, CHUNKS, part + 1, tile, LANES), I16),
            vmem((rows, tile, LANES), F32),
            vmem((rows, tile, LANES), F32),
            vmem((rows, tile, LANES), F32),
            vmem((shards, heads * layers, LANES), F32),
            dma((4,)),
            dma((5,)),
            dma,
            dma((READERS - 1, CHUNKS)),
            dma,
            dma((READERS - 1, CHUNKS)),
            dma,
            dma,
        ],
        compiler_params=pltpu.CompilerParams(
            collective_id=0, has_side_effects=True, vmem_limit_bytes=32 * 2**20
        ),
        cost_estimate=pl.CostEstimate(flops=2**26, bytes_accessed=5 * 2**20, transcendentals=2**19),
    )(
        *(pltpu.with_memory_space_constraint(x, pltpu.HBM) for x in (prefill_states,
        prompt_slot.reshape(1, prompts),
        sample_prompt.reshape(1, rows),
        tiles(queries, rows, heads),
        tiles(keys, rows, heads),
        tiles(values, rows, heads),
        tiles(gates, rows, heads),
        gain, decay_rate)),
    )
    out = out.reshape(rows, STEPS, heads, LAYERS, LANES).transpose(0, 1, 3, 2, 4)
    return out.reshape(rows, STEPS, LAYERS, heads * LANES)


def solution(mesh):
    return jax.shard_map(
        local,
        mesh=mesh,
        in_specs=(
            P("dp", None, "tensor", None, None),
            P(),
            P("dp"),
            P("dp", None, None, "tensor"),
            P("dp", None, None, "tensor"),
            P("dp", None, None, "tensor"),
            P("dp", None, None, "tensor"),
            P(None, "tensor"),
            P(None, "tensor"),
        ),
        out_specs=P("dp", None, None, "tensor"),
        check_vma=False,
    )
```

```python
import functools

import jax
import jax.numpy as jnp
from jax import lax
from jax.experimental import pallas as pl
from jax.experimental.pallas import tpu as pltpu
from jax.sharding import PartitionSpec as P

STEPS = 2
LAYERS = 2
READERS = 4
CHUNKS = 2
LANES = 128
TOP = 32767.0
FINE = 256.0
BATCH = 16
MESH = pl.DeviceIdType.MESH
F32, BF16, I32, I16 = jnp.float32, jnp.bfloat16, jnp.int32, jnp.int16


def iota(shape, axis):
    return lax.broadcasted_iota(I32, shape, axis)


def places(group, groups, owned, copies, sample_prompt, prompt_slot):
    prompts, rows = prompt_slot.shape[1], sample_prompt.shape[1]
    match = (iota((prompts, rows), 0) == sample_prompt).astype(F32).astype(BF16)
    slot_row = jnp.broadcast_to(prompt_slot.astype(F32), (8, prompts)).astype(BF16)
    slots = jnp.dot(slot_row, match, preferred_element_type=F32).astype(I32)[0:1]
    owner, within = slots // owned, slots % owned
    reach = ((group - owner + groups) % groups) // (groups // READERS)
    candidate = reach * owned + within
    count = READERS * owned
    mine = iota((count, rows), 0) == candidate
    earlier = (iota((rows, rows), 0) < iota((rows, rows), 1)).astype(F32).astype(BF16)
    before = jnp.dot(mine.astype(F32).astype(BF16), earlier, preferred_element_type=F32)
    rank = jnp.sum(jnp.where(mine, before, 0.0), axis=0, keepdims=True).astype(I32)
    place = jnp.clip(candidate * copies + rank, 0, rows - 1)
    at = (iota((rows, rows), 0) == place).astype(F32).astype(BF16)
    number = iota((8, rows), 1).astype(F32).astype(BF16)
    order = lax.dot_general(number, at, (((1,), (1,)), ((), ())), preferred_element_type=F32)
    order = jnp.clip(order.astype(I32), 0, rows - 1)
    return jnp.where(iota((8, rows), 0) == 0, order, jnp.broadcast_to(place, (8, rows)))


def kernel(
    groups,
    shards,
    states_hbm,
    slot_hbm,
    prompt_hbm,
    queries_hbm,
    keys_hbm,
    values_hbm,
    gates_hbm,
    gain_hbm,
    decay_hbm,
    out_ref,
    states,
    slot_row,
    prompt_row,
    queries,
    rest,
    gain,
    index_vmem,
    index,
    decay_ref,
    sorted_q,
    arrived_q,
    spread_q,
    products,
    codes_out,
    codes_in,
    local_part,
    gated,
    mixed,
    squares,
    small_sem,
    big_sem,
    query_send,
    query_recv,
    code_send,
    code_recv,
    square_send,
    square_recv,
):
    group, shard = lax.axis_index("dp"), lax.axis_index("tensor")
    quarter = groups // READERS
    owned, layers, heads = states.shape[:3]
    rows, tile = queries.shape[:2]
    pairs = heads * layers
    block = rows // READERS
    part = block // CHUNKS
    copies = block // owned
    part_prompts = owned // CHUNKS

    def reader(r):
        return (lax.rem(group + quarter * r, groups), shard)

    others = [(group, lax.rem(shard + k, shards)) for k in range(1, shards)]

    first = [
        pltpu.make_async_copy(prompt_hbm, prompt_row, small_sem.at[0]),
        pltpu.make_async_copy(slot_hbm, slot_row, small_sem.at[1]),
    ]
    take_q = pltpu.make_async_copy(queries_hbm, queries, big_sem.at[0])
    take_states = pltpu.make_async_copy(states_hbm, states, big_sem.at[1])
    later = [
        pltpu.make_async_copy(ref, rest.at[n], big_sem.at[2 + n])
        for n, ref in enumerate((keys_hbm, values_hbm, gates_hbm))
    ]
    take_gain = pltpu.make_async_copy(gain_hbm, gain, small_sem.at[2])
    take_decay = pltpu.make_async_copy(decay_hbm, decay_ref, small_sem.at[3])
    for copy in (*first, take_q, take_states, *later, take_gain, take_decay):
        copy.start()

    barrier = pltpu.get_barrier_semaphore()
    met = [reader(r) for r in range(1, READERS)] + others
    for device in met:
        pl.semaphore_signal(barrier, inc=1, device_id=device, device_id_type=MESH)

    for copy in first:
        copy.wait()
    index_vmem[...] = places(group, groups, owned, copies, prompt_row[...], slot_row[...])
    take_index = pltpu.make_async_copy(index_vmem, index, small_sem.at[0])
    take_index.start()
    take_index.wait()
    take_q.wait()

    def at_index(which, n):
        return jnp.clip(index[which, n], 0, rows - 1)

    def gather(start, count):
        def step(n, carry):
            sorted_q[start + n] = queries[at_index(0, start + n)]
            return carry

        lax.fori_loop(0, count, step, 0, unroll=8)

    def query_copy(r, c):
        return pltpu.make_async_remote_copy(
            src_ref=sorted_q.at[pl.ds(r * block + c * part, part)],
            dst_ref=arrived_q.at[r - 1, pl.ds(c * part, part)],
            send_sem=query_send,
            recv_sem=query_recv.at[r - 1, c],
            device_id=reader(READERS - r),
            device_id_type=MESH,
        )

    def code_copy(r, c):
        return pltpu.make_async_remote_copy(
            src_ref=codes_out.at[r - 1, c],
            dst_ref=codes_in.at[r - 1, c],
            send_sem=code_send,
            recv_sem=code_recv.at[r - 1, c],
            device_id=reader(r),
            device_id_type=MESH,
        )

    hops = (1, 3, 2)
    met_all = False
    for c in range(CHUNKS):
        for r in hops:
            gather(r * block + c * part, part)
            if not met_all:
                pl.semaphore_wait(barrier, len(met))
                met_all = True
            query_copy(r, c).start()
    gather(0, block)

    def multiply(blocks, c):
        size = copies * tile
        for n, ref in enumerate(blocks):
            wide = ref[...].astype(F32).reshape(part * tile, LANES)
            spread_q[n, pl.ds(0, part * tile)] = wide

        for p in range(part_prompts):
            for pair in range(pairs):
                some = pl.ds(p * size + pair, copies * STEPS, stride=pairs)
                left = [spread_q[n, some, :] for n in range(len(blocks))]
                left = jnp.concatenate(left, axis=0) if len(left) > 1 else left[0]
                state = states[c * part_prompts + p, pair % layers, pair // layers]
                answer = jnp.dot(left.astype(BF16), state, preferred_element_type=F32)
                for n in range(len(blocks)):
                    products[n, some, :] = answer[n * copies * STEPS : (n + 1) * copies * STEPS]

    height = BATCH * tile
    lane = iota((tile, LANES), 1)
    skew = jnp.concatenate([lane - n for n in range(BATCH)], axis=0)
    ones = jnp.ones((2 * LANES, LANES), F32).astype(BF16)
    first_lanes = jnp.where(skew == 0, 1.0, 0.0).astype(BF16)
    first_lanes = jnp.concatenate([first_lanes, first_lanes], axis=1)

    def halves(wide):
        high = wide.astype(BF16)
        low = (wide - high.astype(F32)).astype(BF16)
        return jnp.concatenate([high, low], axis=1)

    def row_sums(wide):
        return jnp.dot(halves(wide), ones, preferred_element_type=F32)

    def spread(columns):
        many = jnp.concatenate([halves(columns)] * BATCH, axis=0) * first_lanes
        return jnp.dot(many, ones, preferred_element_type=F32)

    def over_tiles(wide):
        return sum(wide[n * tile : (n + 1) * tile] for n in range(BATCH))

    def batches(count, step, carry):
        return lax.fori_loop(0, count // BATCH, lambda b, had: step(b * BATCH, had), carry)

    def some_products(n, j):
        return products[n, pl.ds(pl.multiple_of(j * tile, height), height), :]

    def encode(n, r, c):
        def step(j, scales):
            here = some_products(n, j)
            most = jnp.maximum(jnp.max(jnp.abs(here), axis=1, keepdims=True), 1e-30)
            scale = jnp.ceil(jnp.log2(most) * FINE + 0.25)
            code = jnp.round(here * (jnp.exp2(scale * (-1.0 / FINE)) * TOP))
            code = code.astype(I32).astype(I16)
            codes_out[r - 1, c, pl.ds(j, BATCH)] = code.reshape(BATCH, tile, LANES)
            return scales + over_tiles(jnp.where(skew == j, scale, 0.0))

        scales = batches(part, step, jnp.zeros((tile, LANES), F32))
        codes_out[r - 1, c, part] = scales.astype(I32).astype(I16)

    take_decay.wait()
    row = iota((pairs, LANES), 0)
    decay = jnp.zeros((pairs, LANES), F32)
    for pair in range(pairs):
        decay = jnp.where(row == pair, decay_ref[pair % layers, pair // layers], decay)
    retain = jnp.exp(-decay)
    kept = jnp.concatenate([retain, retain * retain], axis=0)
    retains = jnp.concatenate([retain] * BATCH, axis=0)
    kept_batch = jnp.concatenate([kept] * BATCH, axis=0)

    def add_up(j, reach, sums):
        total = reach + local_part[pl.ds(j, BATCH)].reshape(height, LANES)
        mixed[pl.ds(j, BATCH)] = total.reshape(BATCH, tile, LANES)
        square = row_sums(total * total)
        for n in range(BATCH):
            here = square[n * tile : (n + 1) * tile]
            sums = jnp.where(lane == at_index(0, j + n), here, sums)
        return sums

    for copy in later:
        copy.wait()
    take_gain.wait()

    def terms(j, carry):
        query = sorted_q[pl.ds(j, BATCH)].astype(F32)
        key, value = (
            jnp.stack([rest[m, at_index(0, j + n)] for n in range(BATCH)]).astype(F32)
            for m in range(2)
        )

        def of(wide, t):
            return wide[:, t * pairs : (t + 1) * pairs].reshape(BATCH * pairs, LANES)

        key_one, value_one = of(key, 0), of(value, 0)
        inner = jnp.concatenate(
            [of(query, 0) * key_one, of(query, 1) * key_one, of(query, 1) * of(key, 1)], axis=0
        )
        inner = row_sums(inner).reshape(3, BATCH * pairs, LANES)
        term_one = inner[0] * value_one
        term_two = inner[1] * retains * value_one + inner[2] * of(value, 1)
        shape = (BATCH, pairs, LANES)
        local_part[pl.ds(j, BATCH), 0:pairs] = term_one.reshape(shape)
        local_part[pl.ds(j, BATCH), pairs:tile] = term_two.reshape(shape)
        gate = rest[2, pl.ds(j, BATCH)].astype(F32)
        gated[pl.ds(j, BATCH)] = gains[None] * jax.nn.sigmoid(gate)
        return carry

    gains = jnp.concatenate([gain[...], gain[...]], axis=0)
    batches(rows, terms, 0)

    take_states.wait()
    sums = jnp.zeros((tile, LANES), F32)
    for c in range(CHUNKS):
        multiply([sorted_q.at[pl.ds(c * part, part)]], c)

        def own(j, sums):
            return add_up(c * part + j, kept_batch * some_products(0, j), sums)

        sums = batches(part, own, sums)

    for c in range(CHUNKS):
        for some in ((1, 3), (2,)):
            for r in some:
                query_copy(r, c).wait_recv()
            multiply([arrived_q.at[r - 1, pl.ds(c * part, part)] for r in some], c)
            for n, r in enumerate(some):
                encode(n, r, c)
                code_copy(r, c).start()

    for c in range(CHUNKS):
        for r in hops:
            code_copy(r, c).wait_recv()
            scales = jnp.exp2(codes_in[r - 1, c, part].astype(I32).astype(F32) * (1.0 / FINE))
            scales = scales * (1.0 / TOP) * kept

            def decode(j, sums):
                code = codes_in[r - 1, c, pl.ds(j, BATCH)].astype(I32).astype(F32)
                reach = code.reshape(height, LANES) * spread(scales)
                return add_up(r * block + c * part + j, reach, sums)

            sums = batches(part, decode, sums)

    total = []
    for t in range(STEPS):
        here = sums[t * pairs : (t + 1) * pairs]
        for n in (pairs // 2, pairs // 4):
            here = here + pltpu.roll(here, n, 0)
        total.append(here)
    late = (row // layers) % STEPS == 1
    squares[0] = jnp.where(late, total[1], total[0])
    sends = []
    for k, device in enumerate(others):
        copy = pltpu.make_async_remote_copy(
            src_ref=squares.at[0],
            dst_ref=squares.at[k + 1],
            send_sem=square_send,
            recv_sem=square_recv,
            device_id=device,
            device_id_type=MESH,
        )
        copy.start()

    def gate_all(j, carry):
        here = jnp.stack([mixed[at_index(1, j + n)] for n in range(BATCH)])
        out_ref[pl.ds(j, BATCH)] = here * gated[pl.ds(j, BATCH)]
        return carry

    batches(rows, gate_all, 0)
    all_but_one = squares.at[pl.ds(1, shards - 1)]
    pltpu.make_async_copy(all_but_one, all_but_one, square_recv).wait()
    whole = squares[0]
    for k in range(1, shards):
        whole = whole + squares[k]
    scale = lax.rsqrt(whole / (shards * heads * LANES) + 1e-05)
    other = pltpu.roll(scale, layers, 0)
    scale = jnp.concatenate([jnp.where(late, other, scale), jnp.where(late, scale, other)], axis=0)

    def finish(j, columns):
        norm = spread(columns).reshape(BATCH, tile, LANES)
        out_ref[pl.ds(j, BATCH)] = out_ref[pl.ds(j, BATCH)] * norm
        return pltpu.roll(columns, LANES - BATCH, 1)

    batches(rows, finish, scale)

    pltpu.make_async_copy(all_but_one, all_but_one, square_send).wait()
    pltpu.make_async_copy(arrived_q, arrived_q, query_send).wait()
    pltpu.make_async_copy(codes_in, codes_in, code_send).wait()


def tiles(array, rows, heads):
    array = array.reshape(rows, STEPS, LAYERS, heads, LANES).transpose(0, 1, 3, 2, 4)
    return array.reshape(rows, STEPS * heads * LAYERS, LANES)


def local(
    prefill_states, prompt_slot, sample_prompt, queries, keys, values, gates, norm_gain, decay_rate
):
    groups, shards = lax.axis_size("dp"), lax.axis_size("tensor")
    owned, layers, heads = prefill_states.shape[:3]
    rows = sample_prompt.shape[0]
    tile = STEPS * heads * layers
    block = rows // READERS
    part = block // CHUNKS
    prompts = prompt_slot.shape[0]
    gain = norm_gain.reshape(layers, heads, LANES).transpose(1, 0, 2).reshape(heads * layers, LANES)
    hbm = pl.BlockSpec(memory_space=pl.ANY)
    vmem = pltpu.VMEM
    dma = pltpu.SemaphoreType.DMA
    out = pl.pallas_call(
        functools.partial(kernel, groups, shards),
        out_shape=jax.ShapeDtypeStruct((rows, tile, LANES), F32),
        in_specs=[hbm] * 9,
        out_specs=pl.BlockSpec(memory_space=pltpu.VMEM),
        scratch_shapes=[
            vmem(prefill_states.shape, BF16),
            vmem((1, prompts), I32),
            vmem((1, rows), I32),
            vmem((rows, tile, LANES), BF16),
            vmem((3, rows, tile, LANES), BF16),
            vmem((heads * layers, LANES), F32),
            vmem((8, rows), I32),
            pltpu.SMEM((8, rows), I32),
            pltpu.SMEM(decay_rate.shape, F32),
            vmem((rows, tile, LANES), BF16),
            vmem((READERS - 1, block, tile, LANES), BF16),
            vmem((2, part * tile + heads * layers * LAYERS * STEPS * 2, LANES), F32),
            vmem((2, part * tile + heads * layers * LAYERS * STEPS * 2, LANES), F32),
            vmem((READERS - 1, CHUNKS, part + 1, tile, LANES), I16),
            vmem((READERS - 1, CHUNKS, part + 1, tile, LANES), I16),
            vmem((rows, tile, LANES), F32),
            vmem((rows, tile, LANES), F32),
            vmem((rows, tile, LANES), F32),
            vmem((shards, heads * layers, LANES), F32),
            dma((4,)),
            dma((5,)),
            dma,
            dma((READERS - 1, CHUNKS)),
            dma,
            dma((READERS - 1, CHUNKS)),
            dma,
            dma,
        ],
        compiler_params=pltpu.CompilerParams(
            collective_id=0, has_side_effects=True, vmem_limit_bytes=32 * 2**20
        ),
        cost_estimate=pl.CostEstimate(flops=2**26, bytes_accessed=5 * 2**20, transcendentals=2**19),
    )(
        *(pltpu.with_memory_space_constraint(x, pltpu.HBM) for x in (prefill_states,
        prompt_slot.reshape(1, prompts),
        sample_prompt.reshape(1, rows),
        tiles(queries, rows, heads),
        tiles(keys, rows, heads),
        tiles(values, rows, heads),
        tiles(gates, rows, heads),
        gain, decay_rate)),
    )
    out = out.reshape(rows, STEPS, heads, LAYERS, LANES).transpose(0, 1, 3, 2, 4)
    return out.reshape(rows, STEPS, LAYERS, heads * LANES)


def solution(mesh):
    return jax.shard_map(
        local,
        mesh=mesh,
        in_specs=(
            P("dp", None, "tensor", None, None),
            P(),
            P("dp"),
            P("dp", None, None, "tensor"),
            P("dp", None, None, "tensor"),
            P("dp", None, None, "tensor"),
            P("dp", None, None, "tensor"),
            P(None, "tensor"),
            P(None, "tensor"),
        ),
        out_specs=P("dp", None, None, "tensor"),
        check_vma=False,
    )
```

```python
import functools

import jax
import jax.numpy as jnp
from jax import lax
from jax.experimental import pallas as pl
from jax.experimental.pallas import tpu as pltpu
from jax.sharding import PartitionSpec as P

STEPS = 2
LAYERS = 2
READERS = 4
CHUNKS = 2
LANES = 128
TOP = 32767.0
FINE = 256.0
BATCH = 16
MESH = pl.DeviceIdType.MESH
F32, BF16, I32, I16 = jnp.float32, jnp.bfloat16, jnp.int32, jnp.int16


def iota(shape, axis):
    return lax.broadcasted_iota(I32, shape, axis)


def bits(size):
    assert size & (size - 1) == 0
    return size.bit_length() - 1


def places(group, groups, owned, copies, sample_prompt, prompt_slot):
    prompts, rows = prompt_slot.shape[1], sample_prompt.shape[1]
    match = (iota((prompts, rows), 0) == sample_prompt).astype(F32).astype(BF16)
    slot_row = jnp.broadcast_to(prompt_slot.astype(F32), (8, prompts)).astype(BF16)
    slots = jnp.dot(slot_row, match, preferred_element_type=F32).astype(I32)[0:1]
    owner, within = slots >> bits(owned), slots & (owned - 1)
    reach = ((group - owner + groups) & (groups - 1)) >> bits(groups // READERS)
    candidate = reach * owned + within
    count = READERS * owned
    mine = iota((count, rows), 0) == candidate
    earlier = (iota((rows, rows), 0) < iota((rows, rows), 1)).astype(F32).astype(BF16)
    before = jnp.dot(mine.astype(F32).astype(BF16), earlier, preferred_element_type=F32)
    rank = jnp.sum(jnp.where(mine, before, 0.0), axis=0, keepdims=True).astype(I32)
    place = jnp.clip(candidate * copies + rank, 0, rows - 1)
    at = (iota((rows, rows), 0) == place).astype(F32).astype(BF16)
    number = iota((8, rows), 1).astype(F32).astype(BF16)
    order = lax.dot_general(number, at, (((1,), (1,)), ((), ())), preferred_element_type=F32)
    order = jnp.clip(order.astype(I32), 0, rows - 1)
    return jnp.where(iota((8, rows), 0) == 0, order, jnp.broadcast_to(place, (8, rows)))


def kernel(
    groups,
    shards,
    states_hbm,
    slot_hbm,
    prompt_hbm,
    queries_hbm,
    keys_hbm,
    values_hbm,
    gates_hbm,
    gain_hbm,
    decay_hbm,
    out_ref,
    states,
    slot_row,
    prompt_row,
    queries,
    rest,
    gain,
    index_vmem,
    index,
    decay_ref,
    sorted_q,
    arrived_q,
    spread_q,
    products,
    codes_out,
    codes_in,
    local_part,
    gated,
    mixed,
    squares,
    small_sem,
    big_sem,
    query_send,
    query_recv,
    code_send,
    code_recv,
    square_send,
    square_recv,
):
    group, shard = lax.axis_index("dp"), lax.axis_index("tensor")
    quarter = groups // READERS
    owned, layers, heads = states.shape[:3]
    rows, tile = queries.shape[:2]
    pairs = heads * layers
    block = rows // READERS
    part = block // CHUNKS
    copies = block // owned
    part_prompts = owned // CHUNKS

    def reader(r):
        return (lax.rem(group + quarter * r, groups), shard)

    others = [(group, lax.rem(shard + k, shards)) for k in range(1, shards)]

    first = [
        pltpu.make_async_copy(prompt_hbm, prompt_row, small_sem.at[0]),
        pltpu.make_async_copy(slot_hbm, slot_row, small_sem.at[1]),
    ]
    take_q = pltpu.make_async_copy(queries_hbm, queries, big_sem.at[0])
    take_states = pltpu.make_async_copy(states_hbm, states, big_sem.at[1])
    later = [
        pltpu.make_async_copy(ref, rest.at[n], big_sem.at[2 + n])
        for n, ref in enumerate((keys_hbm, values_hbm, gates_hbm))
    ]
    take_gain = pltpu.make_async_copy(gain_hbm, gain, small_sem.at[2])
    take_decay = pltpu.make_async_copy(decay_hbm, decay_ref, small_sem.at[3])
    for copy in first:
        copy.start()
    barrier = pltpu.get_barrier_semaphore()
    met = [reader(r) for r in range(1, READERS)] + others
    for n, device in enumerate(met):
        pl.semaphore_signal(barrier, inc=1, device_id=device, device_id_type=MESH)
        if n == READERS - 2:
            take_q.start()
    for copy in (take_states, *later, take_gain, take_decay):
        copy.start()

    for copy in first:
        copy.wait()
    index_vmem[...] = places(group, groups, owned, copies, prompt_row[...], slot_row[...])
    take_index = pltpu.make_async_copy(index_vmem, index, small_sem.at[0])
    take_index.start()
    take_index.wait()
    take_q.wait()

    def at_index(which, n):
        return jnp.clip(index[which, n], 0, rows - 1)

    def gather(start, count):
        def step(n, carry):
            sorted_q[start + n] = queries[at_index(0, start + n)]
            return carry

        lax.fori_loop(0, count, step, 0, unroll=8)

    def query_copy(r, c):
        return pltpu.make_async_remote_copy(
            src_ref=sorted_q.at[pl.ds(r * block + c * part, part)],
            dst_ref=arrived_q.at[r - 1, pl.ds(c * part, part)],
            send_sem=query_send,
            recv_sem=query_recv.at[r - 1, c],
            device_id=reader(READERS - r),
            device_id_type=MESH,
        )

    def code_copy(r, c):
        return pltpu.make_async_remote_copy(
            src_ref=codes_out.at[r - 1, c],
            dst_ref=codes_in.at[r - 1, c],
            send_sem=code_send,
            recv_sem=code_recv.at[r - 1, c],
            device_id=reader(r),
            device_id_type=MESH,
        )

    hops = (2, 1, 3)
    met_all = False
    for c in range(CHUNKS):
        for r in hops:
            gather(r * block + c * part, part)
            if not met_all:
                pl.semaphore_wait(barrier, len(met))
                met_all = True
            query_copy(r, c).start()
    gather(0, block)

    def multiply(blocks, c):
        size = copies * tile
        for n, ref in enumerate(blocks):
            wide = ref[...].astype(F32).reshape(part * tile, LANES)
            spread_q[n, pl.ds(0, part * tile)] = wide

        for p in range(part_prompts):
            for pair in range(pairs):
                some = pl.ds(p * size + pair, copies * STEPS, stride=pairs)
                left = [spread_q[n, some, :] for n in range(len(blocks))]
                left = jnp.concatenate(left, axis=0) if len(left) > 1 else left[0]
                state = states[c * part_prompts + p, pair % layers, pair // layers]
                answer = jnp.dot(left.astype(BF16), state, preferred_element_type=F32)
                for n in range(len(blocks)):
                    products[n, some, :] = answer[n * copies * STEPS : (n + 1) * copies * STEPS]

    height = BATCH * tile
    lane = iota((tile, LANES), 1)
    skew = jnp.concatenate([lane - n for n in range(BATCH)], axis=0)
    ones = jnp.ones((2 * LANES, LANES), F32).astype(BF16)
    first_lanes = jnp.where(skew == 0, 1.0, 0.0).astype(BF16)
    first_lanes = jnp.concatenate([first_lanes, first_lanes], axis=1)

    def halves(wide):
        high = wide.astype(BF16)
        low = (wide - high.astype(F32)).astype(BF16)
        return jnp.concatenate([high, low], axis=1)

    def row_sums(wide):
        return jnp.dot(halves(wide), ones, preferred_element_type=F32)

    def spread(columns):
        many = jnp.concatenate([halves(columns)] * BATCH, axis=0) * first_lanes
        return jnp.dot(many, ones, preferred_element_type=F32)

    def over_tiles(wide):
        return sum(wide[n * tile : (n + 1) * tile] for n in range(BATCH))

    def batches(count, step, carry):
        return lax.fori_loop(0, count // BATCH, lambda b, had: step(b * BATCH, had), carry)

    def some_products(n, j):
        return products[n, pl.ds(pl.multiple_of(j * tile, height), height), :]

    def encode(n, r, c):
        def step(j, scales):
            here = some_products(n, j)
            most = jnp.maximum(jnp.max(jnp.abs(here), axis=1, keepdims=True), 1e-30)
            scale = jnp.ceil(jnp.log2(most) * FINE + 0.25)
            code = jnp.round(here * (jnp.exp2(scale * (-1.0 / FINE)) * TOP))
            code = code.astype(I32).astype(I16)
            codes_out[r - 1, c, pl.ds(j, BATCH)] = code.reshape(BATCH, tile, LANES)
            return scales + over_tiles(jnp.where(skew == j, scale, 0.0))

        scales = batches(part, step, jnp.zeros((tile, LANES), F32))
        codes_out[r - 1, c, part] = scales.astype(I32).astype(I16)

    take_decay.wait()
    row = iota((pairs, LANES), 0)
    decay = jnp.zeros((pairs, LANES), F32)
    for pair in range(pairs):
        decay = jnp.where(row == pair, decay_ref[pair % layers, pair // layers], decay)
    retain = jnp.exp(-decay)
    kept = jnp.concatenate([retain, retain * retain], axis=0)
    retains = jnp.concatenate([retain] * BATCH, axis=0)
    kept_batch = jnp.concatenate([kept] * BATCH, axis=0)

    def add_up(j, reach, sums):
        total = reach + local_part[pl.ds(j, BATCH)].reshape(height, LANES)
        mixed[pl.ds(j, BATCH)] = total.reshape(BATCH, tile, LANES)
        square = row_sums(total * total)
        for n in range(BATCH):
            here = square[n * tile : (n + 1) * tile]
            sums = jnp.where(lane == at_index(0, j + n), here, sums)
        return sums

    for copy in later:
        copy.wait()
    take_gain.wait()

    def terms(j, carry):
        query = sorted_q[pl.ds(j, BATCH)].astype(F32)
        key, value = (
            jnp.stack([rest[m, at_index(0, j + n)] for n in range(BATCH)]).astype(F32)
            for m in range(2)
        )

        def of(wide, t):
            return wide[:, t * pairs : (t + 1) * pairs].reshape(BATCH * pairs, LANES)

        key_one, value_one = of(key, 0), of(value, 0)
        inner = jnp.concatenate(
            [of(query, 0) * key_one, of(query, 1) * key_one, of(query, 1) * of(key, 1)], axis=0
        )
        inner = row_sums(inner).reshape(3, BATCH * pairs, LANES)
        term_one = inner[0] * value_one
        term_two = inner[1] * retains * value_one + inner[2] * of(value, 1)
        shape = (BATCH, pairs, LANES)
        local_part[pl.ds(j, BATCH), 0:pairs] = term_one.reshape(shape)
        local_part[pl.ds(j, BATCH), pairs:tile] = term_two.reshape(shape)
        gate = rest[2, pl.ds(j, BATCH)].astype(F32)
        gated[pl.ds(j, BATCH)] = gains[None] * jax.nn.sigmoid(gate)
        return carry

    gains = jnp.concatenate([gain[...], gain[...]], axis=0)
    batches(rows, terms, 0)

    take_states.wait()
    sums = jnp.zeros((tile, LANES), F32)
    for c in range(CHUNKS):
        multiply([sorted_q.at[pl.ds(c * part, part)]], c)

        def own(j, sums):
            return add_up(c * part + j, kept_batch * some_products(0, j), sums)

        sums = batches(part, own, sums)

    for c in range(CHUNKS):
        for some in ((2,), (1, 3)):
            for r in some:
                query_copy(r, c).wait_recv()
            multiply([arrived_q.at[r - 1, pl.ds(c * part, part)] for r in some], c)
            for n, r in enumerate(some):
                encode(n, r, c)
                code_copy(r, c).start()

    for c in range(CHUNKS):
        for r in hops:
            code_copy(r, c).wait_recv()
            scales = jnp.exp2(codes_in[r - 1, c, part].astype(I32).astype(F32) * (1.0 / FINE))
            scales = scales * (1.0 / TOP) * kept

            def decode(j, sums):
                code = codes_in[r - 1, c, pl.ds(j, BATCH)].astype(I32).astype(F32)
                reach = code.reshape(height, LANES) * spread(scales)
                return add_up(r * block + c * part + j, reach, sums)

            sums = batches(part, decode, sums)

    total = []
    for t in range(STEPS):
        here = sums[t * pairs : (t + 1) * pairs]
        for n in (pairs // 2, pairs // 4):
            here = here + pltpu.roll(here, n, 0)
        total.append(here)
    late = (row // layers) % STEPS == 1
    squares[0] = jnp.where(late, total[1], total[0])
    sends = []
    for k, device in enumerate(others):
        copy = pltpu.make_async_remote_copy(
            src_ref=squares.at[0],
            dst_ref=squares.at[k + 1],
            send_sem=square_send,
            recv_sem=square_recv,
            device_id=device,
            device_id_type=MESH,
        )
        copy.start()

    def gate_all(j, carry):
        here = jnp.stack([mixed[at_index(1, j + n)] for n in range(BATCH)])
        out_ref[pl.ds(j, BATCH)] = here * gated[pl.ds(j, BATCH)]
        return carry

    batches(rows, gate_all, 0)
    all_but_one = squares.at[pl.ds(1, shards - 1)]
    pltpu.make_async_copy(all_but_one, all_but_one, square_recv).wait()
    whole = squares[0]
    for k in range(1, shards):
        whole = whole + squares[k]
    scale = lax.rsqrt(whole / (shards * heads * LANES) + 1e-05)
    other = pltpu.roll(scale, layers, 0)
    scale = jnp.concatenate([jnp.where(late, other, scale), jnp.where(late, scale, other)], axis=0)

    for j in range(0, rows, BATCH):
        norm = spread(pltpu.roll(scale, LANES - j, 1) if j else scale)
        out_ref[pl.ds(j, BATCH)] = out_ref[pl.ds(j, BATCH)] * norm.reshape(BATCH, tile, LANES)

    pltpu.make_async_copy(all_but_one, all_but_one, square_send).wait()
    pltpu.make_async_copy(arrived_q, arrived_q, query_send).wait()
    pltpu.make_async_copy(codes_in, codes_in, code_send).wait()


def tiles(array, rows, heads):
    array = array.reshape(rows, STEPS, LAYERS, heads, LANES).transpose(0, 1, 3, 2, 4)
    return array.reshape(rows, STEPS * heads * LAYERS, LANES)


def local(
    prefill_states, prompt_slot, sample_prompt, queries, keys, values, gates, norm_gain, decay_rate
):
    groups, shards = lax.axis_size("dp"), lax.axis_size("tensor")
    owned, layers, heads = prefill_states.shape[:3]
    rows = sample_prompt.shape[0]
    tile = STEPS * heads * layers
    block = rows // READERS
    part = block // CHUNKS
    prompts = prompt_slot.shape[0]
    gain = norm_gain.reshape(layers, heads, LANES).transpose(1, 0, 2).reshape(heads * layers, LANES)
    hbm = pl.BlockSpec(memory_space=pl.ANY)
    vmem = pltpu.VMEM
    dma = pltpu.SemaphoreType.DMA
    out = pl.pallas_call(
        functools.partial(kernel, groups, shards),
        out_shape=jax.ShapeDtypeStruct((rows, tile, LANES), F32),
        in_specs=[hbm] * 9,
        out_specs=pl.BlockSpec(memory_space=pltpu.VMEM),
        scratch_shapes=[
            vmem(prefill_states.shape, BF16),
            vmem((1, prompts), I32),
            vmem((1, rows), I32),
            vmem((rows, tile, LANES), BF16),
            vmem((3, rows, tile, LANES), BF16),
            vmem((heads * layers, LANES), F32),
            vmem((8, rows), I32),
            pltpu.SMEM((8, rows), I32),
            pltpu.SMEM(decay_rate.shape, F32),
            vmem((rows, tile, LANES), BF16),
            vmem((READERS - 1, block, tile, LANES), BF16),
            vmem((2, part * tile + heads * layers * LAYERS * STEPS * 2, LANES), F32),
            vmem((2, part * tile + heads * layers * LAYERS * STEPS * 2, LANES), F32),
            vmem((READERS - 1, CHUNKS, part + 1, tile, LANES), I16),
            vmem((READERS - 1, CHUNKS, part + 1, tile, LANES), I16),
            vmem((rows, tile, LANES), F32),
            vmem((rows, tile, LANES), F32),
            vmem((rows, tile, LANES), F32),
            vmem((shards, heads * layers, LANES), F32),
            dma((4,)),
            dma((5,)),
            dma,
            dma((READERS - 1, CHUNKS)),
            dma,
            dma((READERS - 1, CHUNKS)),
            dma,
            dma,
        ],
        compiler_params=pltpu.CompilerParams(
            collective_id=0, has_side_effects=True, vmem_limit_bytes=32 * 2**20
        ),
        cost_estimate=pl.CostEstimate(flops=2**26, bytes_accessed=5 * 2**20, transcendentals=2**19),
    )(
        *(pltpu.with_memory_space_constraint(x, pltpu.HBM) for x in (prefill_states,
        prompt_slot.reshape(1, prompts),
        sample_prompt.reshape(1, rows),
        tiles(queries, rows, heads),
        tiles(keys, rows, heads),
        tiles(values, rows, heads),
        tiles(gates, rows, heads),
        gain, decay_rate)),
    )
    out = out.reshape(rows, STEPS, heads, LAYERS, LANES).transpose(0, 1, 3, 2, 4)
    return out.reshape(rows, STEPS, LAYERS, heads * LANES)


def solution(mesh):
    return jax.shard_map(
        local,
        mesh=mesh,
        in_specs=(
            P("dp", None, "tensor", None, None),
            P(),
            P("dp"),
            P("dp", None, None, "tensor"),
            P("dp", None, None, "tensor"),
            P("dp", None, None, "tensor"),
            P("dp", None, None, "tensor"),
            P(None, "tensor"),
            P(None, "tensor"),
        ),
        out_specs=P("dp", None, None, "tensor"),
        check_vma=False,
    )
```

```python
import functools

import jax
import jax.numpy as jnp
from jax import lax
from jax.experimental import pallas as pl
from jax.experimental.pallas import tpu as pltpu
from jax.sharding import PartitionSpec as P

STEPS = 2
LAYERS = 2
READERS = 4
CHUNKS = 2
LANES = 128
TOP = 32767.0
FINE = 256.0
BATCH = 16
MESH = pl.DeviceIdType.MESH
F32, BF16, I32, I16 = jnp.float32, jnp.bfloat16, jnp.int32, jnp.int16


def iota(shape, axis):
    return lax.broadcasted_iota(I32, shape, axis)


def bits(size):
    assert size & (size - 1) == 0
    return size.bit_length() - 1


def places(group, groups, owned, copies, sample_prompt, prompt_slot):
    prompts, rows = prompt_slot.shape[1], sample_prompt.shape[1]
    match = (iota((prompts, rows), 0) == sample_prompt).astype(F32).astype(BF16)
    slot_row = jnp.broadcast_to(prompt_slot.astype(F32), (8, prompts)).astype(BF16)
    slots = jnp.dot(slot_row, match, preferred_element_type=F32).astype(I32)[0:1]
    owner, within = slots >> bits(owned), slots & (owned - 1)
    reach = ((group - owner + groups) & (groups - 1)) >> bits(groups // READERS)
    candidate = reach * owned + within
    count = READERS * owned
    mine = iota((count, rows), 0) == candidate
    earlier = (iota((rows, rows), 0) < iota((rows, rows), 1)).astype(F32).astype(BF16)
    before = jnp.dot(mine.astype(F32).astype(BF16), earlier, preferred_element_type=F32)
    rank = jnp.sum(jnp.where(mine, before, 0.0), axis=0, keepdims=True).astype(I32)
    place = jnp.clip(candidate * copies + rank, 0, rows - 1)
    at = (iota((rows, rows), 0) == place).astype(F32).astype(BF16)
    number = iota((8, rows), 1).astype(F32).astype(BF16)
    order = lax.dot_general(number, at, (((1,), (1,)), ((), ())), preferred_element_type=F32)
    order = jnp.clip(order.astype(I32), 0, rows - 1)
    return jnp.where(iota((8, rows), 0) == 0, order, jnp.broadcast_to(place, (8, rows)))


def kernel(
    groups,
    shards,
    states_hbm,
    slot_hbm,
    prompt_hbm,
    queries_hbm,
    keys_hbm,
    values_hbm,
    gates_hbm,
    gain_hbm,
    decay_hbm,
    out_ref,
    states,
    slot_row,
    prompt_row,
    queries,
    rest,
    gain,
    index_vmem,
    index,
    decay_ref,
    sorted_q,
    arrived_q,
    spread_q,
    products,
    codes_out,
    codes_in,
    local_part,
    gated,
    mixed,
    squares,
    small_sem,
    big_sem,
    query_send,
    query_recv,
    code_send,
    code_recv,
    square_send,
    square_recv,
):
    group, shard = lax.axis_index("dp"), lax.axis_index("tensor")
    quarter = groups // READERS
    owned, layers, heads = states.shape[:3]
    rows, tile = queries.shape[:2]
    pairs = heads * layers
    block = rows // READERS
    part = block // CHUNKS
    copies = block // owned
    part_prompts = owned // CHUNKS

    def reader(r):
        return ((group + quarter * r) & (groups - 1), shard)

    others = [k + (shard <= k).astype(I32) for k in range(shards - 1)]

    first = [
        pltpu.make_async_copy(prompt_hbm, prompt_row, small_sem.at[0]),
        pltpu.make_async_copy(slot_hbm, slot_row, small_sem.at[1]),
    ]
    take_q = pltpu.make_async_copy(queries_hbm, queries, big_sem.at[0])
    take_states = pltpu.make_async_copy(states_hbm, states, big_sem.at[1])
    later = [
        pltpu.make_async_copy(ref, rest.at[n], big_sem.at[2 + n])
        for n, ref in enumerate((keys_hbm, values_hbm, gates_hbm))
    ]
    take_gain = pltpu.make_async_copy(gain_hbm, gain, small_sem.at[2])
    take_decay = pltpu.make_async_copy(decay_hbm, decay_ref, small_sem.at[3])
    for copy in first:
        copy.start()
    barrier = pltpu.get_barrier_semaphore()
    met = [reader(r) for r in range(1, READERS)]
    met += [(group, other) for other in others]
    for n, device in enumerate(met):
        pl.semaphore_signal(barrier, inc=1, device_id=device, device_id_type=MESH)
        if n == READERS - 2:
            take_q.start()
    for copy in (take_states, *later, take_gain, take_decay):
        copy.start()

    for copy in first:
        copy.wait()
    index_vmem[...] = places(group, groups, owned, copies, prompt_row[...], slot_row[...])
    take_index = pltpu.make_async_copy(index_vmem, index, small_sem.at[0])
    take_index.start()
    take_index.wait()
    take_q.wait()

    def at_index(which, n):
        return jnp.clip(index[which, n], 0, rows - 1)

    def gather(start, count):
        def step(n, carry):
            sorted_q[start + n] = queries[at_index(0, start + n)]
            return carry

        lax.fori_loop(0, count, step, 0, unroll=8)

    def query_copy(r, c):
        return pltpu.make_async_remote_copy(
            src_ref=sorted_q.at[pl.ds(r * block + c * part, part)],
            dst_ref=arrived_q.at[r - 1, pl.ds(c * part, part)],
            send_sem=query_send,
            recv_sem=query_recv.at[r - 1, c],
            device_id=reader(READERS - r),
            device_id_type=MESH,
        )

    def code_copy(r, c):
        return pltpu.make_async_remote_copy(
            src_ref=codes_out.at[r - 1, c],
            dst_ref=codes_in.at[r - 1, c],
            send_sem=code_send,
            recv_sem=code_recv.at[r - 1, c],
            device_id=reader(r),
            device_id_type=MESH,
        )

    hops = (2, 1, 3)
    for r in hops:
        gather(r * block, part)
    pl.semaphore_wait(barrier, len(met))
    for c in range(CHUNKS):
        for r in hops:
            if c:
                gather(r * block + c * part, part)
            query_copy(r, c).start()
    gather(0, block)

    def multiply(blocks, c):
        size = copies * tile
        for n, ref in enumerate(blocks):
            wide = ref[...].astype(F32).reshape(part * tile, LANES)
            spread_q[n, pl.ds(0, part * tile)] = wide

        for p in range(part_prompts):
            for pair in range(pairs):
                some = pl.ds(p * size + pair, copies * STEPS, stride=pairs)
                left = [spread_q[n, some, :] for n in range(len(blocks))]
                left = jnp.concatenate(left, axis=0) if len(left) > 1 else left[0]
                state = states[c * part_prompts + p, pair % layers, pair // layers]
                answer = jnp.dot(left.astype(BF16), state, preferred_element_type=F32)
                for n in range(len(blocks)):
                    products[n, some, :] = answer[n * copies * STEPS : (n + 1) * copies * STEPS]

    height = BATCH * tile
    lane = iota((tile, LANES), 1)
    skew = jnp.concatenate([lane - n for n in range(BATCH)], axis=0)
    ones = jnp.ones((2 * LANES, LANES), F32).astype(BF16)
    first_lanes = jnp.where(skew == 0, 1.0, 0.0).astype(BF16)
    first_lanes = jnp.concatenate([first_lanes, first_lanes], axis=1)

    def halves(wide):
        high = wide.astype(BF16)
        low = (wide - high.astype(F32)).astype(BF16)
        return jnp.concatenate([high, low], axis=1)

    def row_sums(wide):
        return jnp.dot(halves(wide), ones, preferred_element_type=F32)

    def spread(columns):
        many = jnp.concatenate([halves(columns)] * BATCH, axis=0) * first_lanes
        return jnp.dot(many, ones, preferred_element_type=F32)

    def over_tiles(wide):
        return sum(wide[n * tile : (n + 1) * tile] for n in range(BATCH))

    def batches(count, step, carry):
        return lax.fori_loop(0, count // BATCH, lambda b, had: step(b * BATCH, had), carry)

    def some_products(n, j):
        return products[n, pl.ds(pl.multiple_of(j * tile, height), height), :]

    def encode(n, r, c):
        def step(j, scales):
            here = some_products(n, j)
            most = jnp.maximum(jnp.max(jnp.abs(here), axis=1, keepdims=True), 1e-30)
            scale = jnp.ceil(jnp.log2(most) * FINE + 0.25)
            code = jnp.round(here * (jnp.exp2(scale * (-1.0 / FINE)) * TOP))
            code = code.astype(I32).astype(I16)
            codes_out[r - 1, c, pl.ds(j, BATCH)] = code.reshape(BATCH, tile, LANES)
            return scales + over_tiles(jnp.where(skew == j, scale, 0.0))

        scales = batches(part, step, jnp.zeros((tile, LANES), F32))
        codes_out[r - 1, c, part] = scales.astype(I32).astype(I16)

    take_decay.wait()
    row = iota((pairs, LANES), 0)
    decay = jnp.zeros((pairs, LANES), F32)
    for pair in range(pairs):
        decay = jnp.where(row == pair, decay_ref[pair % layers, pair // layers], decay)
    retain = jnp.exp(-decay)
    kept = jnp.concatenate([retain, retain * retain], axis=0)
    retains = jnp.concatenate([retain] * BATCH, axis=0)
    kept_batch = jnp.concatenate([kept] * BATCH, axis=0)

    def add_up(j, reach, sums):
        total = reach + local_part[pl.ds(j, BATCH)].reshape(height, LANES)
        mixed[pl.ds(j, BATCH)] = total.reshape(BATCH, tile, LANES)
        square = row_sums(total * total)
        for n in range(BATCH):
            here = square[n * tile : (n + 1) * tile]
            sums = jnp.where(lane == at_index(0, j + n), here, sums)
        return sums

    for copy in later:
        copy.wait()
    take_gain.wait()

    def terms(j, carry):
        query = sorted_q[pl.ds(j, BATCH)].astype(F32)
        key, value = (
            jnp.stack([rest[m, at_index(0, j + n)] for n in range(BATCH)]).astype(F32)
            for m in range(2)
        )

        def of(wide, t):
            return wide[:, t * pairs : (t + 1) * pairs].reshape(BATCH * pairs, LANES)

        key_one, value_one = of(key, 0), of(value, 0)
        inner = jnp.concatenate(
            [of(query, 0) * key_one, of(query, 1) * key_one, of(query, 1) * of(key, 1)], axis=0
        )
        inner = row_sums(inner).reshape(3, BATCH * pairs, LANES)
        term_one = inner[0] * value_one
        term_two = inner[1] * retains * value_one + inner[2] * of(value, 1)
        shape = (BATCH, pairs, LANES)
        local_part[pl.ds(j, BATCH), 0:pairs] = term_one.reshape(shape)
        local_part[pl.ds(j, BATCH), pairs:tile] = term_two.reshape(shape)
        gate = rest[2, pl.ds(j, BATCH)].astype(F32)
        gated[pl.ds(j, BATCH)] = gains[None] * jax.nn.sigmoid(gate)
        return carry

    gains = jnp.concatenate([gain[...], gain[...]], axis=0)
    batches(rows, terms, 0)

    take_states.wait()
    sums = jnp.zeros((tile, LANES), F32)
    for c in range(CHUNKS):
        multiply([sorted_q.at[pl.ds(c * part, part)]], c)

        def own(j, sums):
            return add_up(c * part + j, kept_batch * some_products(0, j), sums)

        sums = batches(part, own, sums)

    for c in range(CHUNKS):
        for some in ((2,), (1, 3)):
            for r in some:
                query_copy(r, c).wait_recv()
            multiply([arrived_q.at[r - 1, pl.ds(c * part, part)] for r in some], c)
            for n, r in enumerate(some):
                encode(n, r, c)
                code_copy(r, c).start()

    for c in range(CHUNKS):
        for r in hops:
            code_copy(r, c).wait_recv()
            scales = jnp.exp2(codes_in[r - 1, c, part].astype(I32).astype(F32) * (1.0 / FINE))
            scales = scales * (1.0 / TOP) * kept

            def decode(j, sums):
                code = codes_in[r - 1, c, pl.ds(j, BATCH)].astype(I32).astype(F32)
                reach = code.reshape(height, LANES) * spread(scales)
                return add_up(r * block + c * part + j, reach, sums)

            sums = batches(part, decode, sums)

    total = []
    for t in range(STEPS):
        here = sums[t * pairs : (t + 1) * pairs]
        for n in (pairs // 2, pairs // 4):
            here = here + pltpu.roll(here, n, 0)
        total.append(here)
    late = (row // layers) % STEPS == 1
    squares[0] = jnp.where(late, total[1], total[0])
    for other in others:
        copy = pltpu.make_async_remote_copy(
            src_ref=squares.at[0],
            dst_ref=squares.at[(other - shard) & (shards - 1)],
            send_sem=square_send,
            recv_sem=square_recv,
            device_id=(group, other),
            device_id_type=MESH,
        )
        copy.start()

    def gate_all(j, carry):
        here = jnp.stack([mixed[at_index(1, j + n)] for n in range(BATCH)])
        out_ref[pl.ds(j, BATCH)] = here * gated[pl.ds(j, BATCH)]
        return carry

    batches(rows, gate_all, 0)
    all_but_one = squares.at[pl.ds(1, shards - 1)]
    pltpu.make_async_copy(all_but_one, all_but_one, square_recv).wait()
    whole = squares[0]
    for k in range(1, shards):
        whole = whole + squares[k]
    scale = lax.rsqrt(whole / (shards * heads * LANES) + 1e-05)
    other = pltpu.roll(scale, layers, 0)
    scale = jnp.concatenate([jnp.where(late, other, scale), jnp.where(late, scale, other)], axis=0)

    for j in range(0, rows, BATCH):
        norm = spread(pltpu.roll(scale, LANES - j, 1) if j else scale)
        out_ref[pl.ds(j, BATCH)] = out_ref[pl.ds(j, BATCH)] * norm.reshape(BATCH, tile, LANES)

    pltpu.make_async_copy(all_but_one, all_but_one, square_send).wait()
    pltpu.make_async_copy(arrived_q, arrived_q, query_send).wait()
    pltpu.make_async_copy(codes_in, codes_in, code_send).wait()


def tiles(array, rows, heads):
    array = array.reshape(rows, STEPS, LAYERS, heads, LANES).transpose(0, 1, 3, 2, 4)
    return array.reshape(rows, STEPS * heads * LAYERS, LANES)


def local(
    prefill_states, prompt_slot, sample_prompt, queries, keys, values, gates, norm_gain, decay_rate
):
    groups, shards = lax.axis_size("dp"), lax.axis_size("tensor")
    owned, layers, heads = prefill_states.shape[:3]
    rows = sample_prompt.shape[0]
    tile = STEPS * heads * layers
    block = rows // READERS
    part = block // CHUNKS
    prompts = prompt_slot.shape[0]
    gain = norm_gain.reshape(layers, heads, LANES).transpose(1, 0, 2).reshape(heads * layers, LANES)
    hbm = pl.BlockSpec(memory_space=pl.ANY)
    vmem = pltpu.VMEM
    dma = pltpu.SemaphoreType.DMA
    out = pl.pallas_call(
        functools.partial(kernel, groups, shards),
        out_shape=jax.ShapeDtypeStruct((rows, tile, LANES), F32),
        in_specs=[hbm] * 9,
        out_specs=pl.BlockSpec(memory_space=pltpu.VMEM),
        scratch_shapes=[
            vmem(prefill_states.shape, BF16),
            vmem((1, prompts), I32),
            vmem((1, rows), I32),
            vmem((rows, tile, LANES), BF16),
            vmem((3, rows, tile, LANES), BF16),
            vmem((heads * layers, LANES), F32),
            vmem((8, rows), I32),
            pltpu.SMEM((8, rows), I32),
            pltpu.SMEM(decay_rate.shape, F32),
            vmem((rows, tile, LANES), BF16),
            vmem((READERS - 1, block, tile, LANES), BF16),
            vmem((2, part * tile + heads * layers * LAYERS * STEPS * 2, LANES), F32),
            vmem((2, part * tile + heads * layers * LAYERS * STEPS * 2, LANES), F32),
            vmem((READERS - 1, CHUNKS, part + 1, tile, LANES), I16),
            vmem((READERS - 1, CHUNKS, part + 1, tile, LANES), I16),
            vmem((rows, tile, LANES), F32),
            vmem((rows, tile, LANES), F32),
            vmem((rows, tile, LANES), F32),
            vmem((shards, heads * layers, LANES), F32),
            dma((4,)),
            dma((5,)),
            dma,
            dma((READERS - 1, CHUNKS)),
            dma,
            dma((READERS - 1, CHUNKS)),
            dma,
            dma,
        ],
        compiler_params=pltpu.CompilerParams(
            collective_id=0, has_side_effects=True, vmem_limit_bytes=32 * 2**20
        ),
        cost_estimate=pl.CostEstimate(flops=2**26, bytes_accessed=5 * 2**20, transcendentals=2**19),
    )(
        *(pltpu.with_memory_space_constraint(x, pltpu.HBM) for x in (prefill_states,
        prompt_slot.reshape(1, prompts),
        sample_prompt.reshape(1, rows),
        tiles(queries, rows, heads),
        tiles(keys, rows, heads),
        tiles(values, rows, heads),
        tiles(gates, rows, heads),
        gain, decay_rate)),
    )
    out = out.reshape(rows, STEPS, heads, LAYERS, LANES).transpose(0, 1, 3, 2, 4)
    return out.reshape(rows, STEPS, LAYERS, heads * LANES)


def solution(mesh):
    return jax.shard_map(
        local,
        mesh=mesh,
        in_specs=(
            P("dp", None, "tensor", None, None),
            P(),
            P("dp"),
            P("dp", None, None, "tensor"),
            P("dp", None, None, "tensor"),
            P("dp", None, None, "tensor"),
            P("dp", None, None, "tensor"),
            P(None, "tensor"),
            P(None, "tensor"),
        ),
        out_specs=P("dp", None, None, "tensor"),
        check_vma=False,
    )
```
